512 devices in a mesh: ex: 128 (over y, x, z_hi), blk: 4 (over z_lo, core).
Axes of the slice: x: 4, y: 8, z: 8 (z_hi: 4, z_lo: 2; z = z_hi * 2 + z_lo), core: 2. Of those that a mesh axis runs over, the one named last changes fastest.
Arguments:
- train_grads: bfloat16 [1024, 10240], P('ex', 'blk'), may hold values from -0.0234375 to 0.0234375
- train_acts: bfloat16 [1024, 2560], P('ex', 'blk'), may hold values from -0.0234375 to 0.0234375
- train_mask: int32 [1024], P('ex'), may hold values 0 or 1
- query_grads: bfloat16 [512, 10240], P('ex', 'blk'), may hold values from -6 to 6
- query_acts: bfloat16 [512, 2560], P('ex', 'blk'), may hold values from -6 to 6
- grad_basis: bfloat16 [10240, 10240], P('blk', 'ex'), may hold values from -0.0625 to 0.0625
- act_basis: bfloat16 [2560, 2560], P('blk', 'ex'), may hold values from -0.125 to 0.125
- eigenvalues: float32 [10240, 2560], P('ex'), may hold values from 0.1 to 10
Outputs:
- scores: float32 [1024, 8], P(('ex', 'blk'))
The draws below stay inside these ranges and needn't reach their ends.
All inputs are finite; a program needn't handle non-finite values. No bound on the sum of `train_mask` on one device may be relied on, other than what follows from the above.
Results may differ from the reference program's by a relative error of at most 0.0039.
Values may be sent and summed in bfloat16 or wider, within the bound.
No kernel may reach another device: no remote copies, remote signals or barrier semaphores. Data moves between devices by JAX's collectives and lax.ppermute only.
A program may use at most 64 MiB of HBM per device.

```python
import math
import jax
import jax.numpy as jnp
from jax import lax

D = 2560
F = 10240
QRY = 8
QLEN = 64
TOKENS = 1024


def with_ends(result, key, smallest, largest):
    longest = result.shape.index(max(result.shape))
    spots = []
    for shift in (0, 1):
        where = [jax.random.randint(jax.random.fold_in(key, axis), (), 0, length) for axis, length in enumerate(result.shape)]
        where[longest] = (where[longest] + shift) % result.shape[longest]
        spots.append(tuple(where))
    return result.at[spots[0]].set(smallest).at[spots[1]].set(largest)


def levels(rng, extent, cuts, least, top_value):
    def one(dim, parts):
        heights = jax.random.uniform(jax.random.fold_in(jax.random.fold_in(rng, 6), dim), (parts,), jnp.float32, least / len(cuts), top_value / len(cuts))
        return jnp.repeat(jnp.exp(heights), extent[dim] // parts).reshape((-1,) + (1,) * (len(extent) - dim - 1))

    level = one(*cuts[0])
    for cut in cuts[1:]:
        level = level * one(*cut)
    return level


def scatter_about(rng, extent, spread, most, cuts=(), held_as=jnp.bfloat16):
    values = jax.random.normal(rng, extent, jnp.float32) * spread
    if len(cuts) > 0:
        values = levels(rng, extent, cuts, -0.22, 0.18) * values
    return jnp.clip(values, min=-most, max=most).astype(held_as)


def setup_inputs(seed: int = 0) -> dict:
    key_list = jax.random.split(jax.random.key(seed), 9)
    return {
        "train_grads": scatter_about(key_list[0], (TOKENS, F), 0.004, 0.0234375, ((0, 128), (1, 4))),
        "train_acts": scatter_about(key_list[1], (TOKENS, D), 0.004, 0.0234375, ((0, 128), (1, 4))),
        "train_mask": with_ends((jax.random.randint(key_list[2], (TOKENS,), 0, 4) < 3).astype(jnp.int32), jax.random.fold_in(key_list[2], 1), 0, 1),
        "query_grads": scatter_about(key_list[3], (QRY * QLEN, F), 1.0, 6.0, ((0, 128), (1, 4))),
        "query_acts": scatter_about(key_list[4], (QRY * QLEN, D), 1.0, 6.0, ((0, 128), (1, 4))),
        "grad_basis": scatter_about(key_list[5], (F, F), F ** -0.5, 0.0625, ((0, 4), (1, 128))),
        "act_basis": scatter_about(key_list[6], (D, D), D ** -0.5, 0.125, ((0, 4), (1, 128))),
        "eigenvalues": jnp.clip(jnp.exp(math.log(10.0) - 4.6051702 * jax.random.uniform(key_list[7], (F, D), jnp.float32) ** levels(key_list[7], (F, D), ((0, 128),), -0.2, 0.2)), 0.1, 10.0),
    }


damping = 0.1


def reference(train_grads, train_acts, train_mask, query_grads, query_acts, grad_basis, act_basis, eigenvalues):
    masked = train_grads * train_mask[:, None].astype(train_grads.dtype)
    train_grad_rot = jnp.dot(masked, grad_basis, preferred_element_type=jnp.float32)
    train_act_rot = jnp.dot(train_acts, act_basis, preferred_element_type=jnp.float32).astype(jnp.bfloat16)
    query_grad_rot = jnp.dot(query_grads, grad_basis, preferred_element_type=jnp.float32).astype(jnp.bfloat16)
    query_act_rot = jnp.dot(query_acts, act_basis, preferred_element_type=jnp.float32).astype(jnp.bfloat16)
    query_grad_rot = query_grad_rot.reshape(QRY, QLEN, F)
    query_act_rot = query_act_rot.reshape(QRY, QLEN, D)
    train_act_wide = train_act_rot.astype(jnp.float32)

    def score_query(pair):
        grads_query, acts_query = pair
        raw_block = jnp.dot(grads_query.T, acts_query, preferred_element_type=jnp.float32)
        scaled = raw_block / (eigenvalues + damping)
        mixed = jnp.dot(train_act_wide, scaled.T, precision=lax.Precision.HIGHEST, preferred_element_type=jnp.float32)
        return jnp.sum(train_grad_rot * mixed, axis=1)

    per_query = lax.map(score_query, (query_grad_rot, query_act_rot))
    return per_query.T
```

```python
import functools

import jax
import jax.numpy as jnp
from jax import lax
from jax.experimental import pallas as pl
from jax.experimental.pallas import tpu as pltpu
from jax.sharding import Mesh, PartitionSpec as P

damping = 0.1

BF = jnp.bfloat16
F32 = jnp.float32


def pick(row_of, rows, cols, dtype=BF):
    r = lax.broadcasted_iota(jnp.int32, (rows, cols), 0)
    c = lax.broadcasted_iota(jnp.int32, (rows, cols), 1)
    return (row_of(r) == c).astype(dtype)


def high_low(v):
    high = v.astype(BF)
    return high, (v - high.astype(F32)).astype(BF)


def swap(v, axis):
    return lax.ppermute(v, axis, [(0, 1), (1, 0)])


def exchange(pieces, axis):
    n = lax.axis_size(axis)
    me = lax.axis_index(axis)
    received = [lax.dynamic_index_in_dim(pieces, me, 0, keepdims=False)]
    for step in range(1, n):
        out = lax.dynamic_index_in_dim(pieces, (me + step) % n, 0, keepdims=False)
        received.append(lax.ppermute(out, axis, [(i, (i + step) % n) for i in range(n)]))
    stacked = jnp.stack(received)
    order = (me - jnp.arange(n)) % n
    return jnp.concatenate(
        [lax.dynamic_index_in_dim(stacked, order[k], 0, keepdims=True) for k in range(n)], 0
    )


def spread(v, axes, count):
    return lax.all_to_all(jnp.broadcast_to(v[None], (count,) + v.shape), axes, 0, 0, tiled=True)


def rotate_kernel(full_ref, g0_ref, g1_ref, a0_ref, a1_ref, out_ref, *, X, H, L, tt, tq, gs, f_own):
    per = 2 * (tt + tq)
    inner = X // L
    wt, wq = inner * tt, inner * tq
    for l in range(L):
        g = a = 0.0
        for s, (bg, ba) in enumerate(((g0_ref, a0_ref), (g1_ref, a1_ref))):
            rows = [full_ref[pl.ds((l * inner + x) * per + s * tt, tt), :] for x in range(inner)]
            rows += [full_ref[pl.ds((l * inner + x) * per + 2 * tt + s * tq, tq), :] for x in range(inner)]
            tokens = jnp.concatenate(rows, 0)
            g += lax.dot_general(bg[...], tokens[:, :gs], (((1,), (1,)), ((), ())), preferred_element_type=F32)
            a += lax.dot_general(ba[...], tokens[:, gs:], (((1,), (1,)), ((), ())), preferred_element_type=F32)
        g_high, g_low = high_low(g[:, wt:])
        g_train = g[:, :wt].astype(BF)
        a_high, a_low = high_low(a)
        for h in range(H):
            m = h * L + l
            out_ref[m, :f_own, :wt] = g_train[h * f_own:(h + 1) * f_own]
            out_ref[m, :f_own, wt:wt + wq] = g_high[h * f_own:(h + 1) * f_own]
            out_ref[m, :f_own, wt + wq:] = g_low[h * f_own:(h + 1) * f_own]
        for m in range(H * L):
            r = slice(m * 16, m * 16 + 16)
            at = f_own + 16 * l
            out_ref[m, at:at + 16, :wt] = a_high[r, :wt]
            out_ref[m, at:at + 16, wt:] = a_low[r, :wt]
            at = f_own + 16 * L
            out_ref[m, at:at + 16, l * 2 * wq:l * 2 * wq + wq] = a_high[r, wt:]
            out_ref[m, at:at + 16, l * 2 * wq + wq:(l + 1) * 2 * wq] = a_low[r, wt:]


def combine_kernel(parts_ref, g_ref, a_ref, *, n, f_own, L, wt, wq, d_part):
    total = parts_ref[0].astype(F32)
    for k in range(1, n):
        total += parts_ref[k].astype(F32)
    g_train = total[:f_own, :wt].astype(BF)
    g_query = (total[:f_own, wt:wt + wq] + total[:f_own, wt + wq:]).astype(BF)
    for k in range(g_ref.shape[0]):
        g_ref[k, :, :wt] = g_train
        g_ref[k, :, wt:] = g_query
    a_train = [total[f_own + 16 * l:f_own + 16 * l + 16] for l in range(L)]
    a_train = jnp.concatenate([t[:, :wt] + t[:, wt:] for t in a_train], 1)
    last = total[f_own + 16 * L:]
    a_query = jnp.concatenate(
        [last[:, l * 2 * wq:l * 2 * wq + wq] + last[:, l * 2 * wq + wq:(l + 1) * 2 * wq] for l in range(L)], 1
    ).astype(BF)
    half = d_part // 2
    r = lax.broadcasted_iota(jnp.int32, (16, 16), 0)
    c = lax.broadcasted_iota(jnp.int32, (16, 16), 1)
    inside = (r >= d_part) & (r < d_part + half)
    sides = [
        jnp.dot((inside & (c == r - d_part + k * half)).astype(BF), a_query, preferred_element_type=F32)
        for k in range(2)
    ]
    packed = (a_train + jnp.concatenate(sides, 1)).astype(BF)
    for k in range(a_ref.shape[0]):
        a_ref[k] = packed


def score_kernel(a_ref, ao_ref, g_ref, go_ref, inv_ref, out_ref, *, Y, H, L, wt, wq, d_part, group):
    half = d_part // 2
    n = a_ref.shape[0]
    r = lax.broadcasted_iota(jnp.int32, (n, n), 0)
    c = lax.broadcasted_iota(jnp.int32, (n, n), 1)
    j = r % 16
    base = r - j + d_part
    unpack = [
        ((j >= k * half) & (j < (k + 1) * half) & (c == base + j - k * half)).astype(BF) for k in range(2)
    ]

    def query_acts(ref):
        width = ref.shape[1] // 2
        return (
            jnp.dot(unpack[0], ref[:, :width], preferred_element_type=F32)
            + jnp.dot(unpack[1], ref[:, width:], preferred_element_type=F32)
        ).astype(BF)

    def grads(ref, cols):
        return jnp.concatenate(
            [jnp.concatenate([ref[h * L + l, :, cols] for h in range(H)], 0) for l in range(L)], 1
        )

    qa = jnp.concatenate([query_acts(a_ref), query_acts(ao_ref)], 1)
    qg = jnp.concatenate([grads(g_ref, slice(wt, wt + wq)), grads(go_ref, slice(wt, wt + wq))], 1)
    g_train = grads(g_ref, slice(0, wt)).astype(F32)
    d_tile = inv_ref.shape[1] // 2
    r = lax.broadcasted_iota(jnp.int32, (d_tile, n), 0)
    c = lax.broadcasted_iota(jnp.int32, (d_tile, n), 1)
    place = (c == (r // d_part) * 16 + r % d_part).astype(BF)
    inv = jnp.dot(inv_ref[:, :d_tile], place, preferred_element_type=F32) + jnp.dot(
        inv_ref[:, d_tile:], place, preferred_element_type=F32
    )
    owner = (lax.broadcasted_iota(jnp.int32, qg.shape, 1) // group) % Y
    acts = a_ref[...]
    for q in range(Y):
        raw = lax.dot_general(
            jnp.where(owner == q, qg, jnp.zeros_like(qg)), qa, (((1,), (1,)), ((), ())), preferred_element_type=F32
        )
        mixed = jnp.dot((raw * inv).astype(BF), acts, preferred_element_type=F32)
        out_ref[q:q + 1, :] = jnp.sum(mixed * g_train, axis=0, keepdims=True)


def local_call(kernel, shapes, *args):
    return pl.pallas_call(
        kernel,
        out_shape=shapes,
        in_specs=[pl.BlockSpec(memory_space=pltpu.VMEM)] * len(args),
        out_specs=jax.tree.map(lambda _: pl.BlockSpec(memory_space=pltpu.VMEM), shapes),
        compiler_params=pltpu.CompilerParams(vmem_limit_bytes=40 * 2**20),
    )(*args)


def per_device(
    train_grads, train_acts, train_mask, query_grads, query_acts, grad_basis, act_basis, eigenvalues
):
    Y, X, H, L, C = (lax.axis_size(a) for a in ("y", "x", "zh", "zl", "c"))
    core = lax.axis_index("c")
    low = lax.axis_index("zl")
    gk, f_own = grad_basis.shape
    ak, d_own = act_basis.shape
    gs, as_ = gk // H, ak // H
    nt, nq = train_grads.shape[0], query_grads.shape[0]
    th, qh = nt // C, nq // C
    d_all = eigenvalues.shape[1]
    f_tile, d_block = f_own * H, d_own * H
    d_part = d_block // (H * L)
    d_tile = d_part * X * Y

    masked = train_grads * train_mask[:, None].astype(BF)
    grads = jnp.concatenate([masked.reshape(L, C, nt // (L * C), gk).transpose(1, 0, 2, 3).reshape(C, th, gk),
                             query_grads.reshape(C, qh, gk)], 1)
    acts = jnp.concatenate([train_acts.reshape(L, C, nt // (L * C), ak).transpose(1, 0, 2, 3).reshape(C, th, ak),
                            query_acts.reshape(C, qh, ak)], 1)
    both = jnp.concatenate([grads, acts], 2)
    mine = jnp.where(core == 0, both[0], both[1])
    theirs = jnp.where(core == 0, both[1], both[0])
    rows2 = jnp.stack([mine, swap(theirs, "c")])

    width = gs + as_
    slices = jnp.concatenate(
        [rows2[:, :, :gk].reshape(C, th + qh, H, gs), rows2[:, :, gk:].reshape(C, th + qh, H, as_)], 3
    ).transpose(2, 0, 1, 3)
    train_rows = slices[:, :, :th].reshape(H, C * th, width)
    query_rows = slices[:, :, th:].reshape(H, C * qh * 2, width // 2)
    message = jnp.concatenate([train_rows, query_rows], 2)
    message = jnp.broadcast_to(message[None], (Y,) + message.shape).reshape((Y * H,) + message.shape[1:])
    got = lax.all_to_all(message, ("y", "zh"), 0, 0, tiled=True)
    got = got.reshape(Y * H * C * th, width + width // 2)

    gb = grad_basis.T.reshape(f_own, H, gs).transpose(1, 0, 2)
    ab = act_basis.T.reshape(d_own, H, as_).transpose(1, 0, 2)
    ab = jnp.pad(ab, ((0, 0), (0, 0), (0, gs - as_)))
    own = exchange(jnp.concatenate([gb, ab], 1), "zh")
    other = swap(own, "c")

    def base(v):
        a = v[:, f_own:, :as_].reshape(H * L, d_part, as_)
        return v[:, :f_own].reshape(f_tile, gs), jnp.pad(a, ((0, 0), (0, 16 - d_part), (0, 0))).reshape(H * L * 16, as_)

    (g0, a0), (g1, a1) = base(own), base(other)

    G = Y * H
    src = C * th

    def train_row(r):
        s, rest = r // (G * th), r % (G * th)
        return (rest // th) * src + s * th + rest % th

    def query_row(half):
        def row(r):
            s, rest = r // (G * qh), r % (G * qh)
            return (rest // qh) * src + (s * qh + rest % qh) * 2 + half
        return row

    def move(row_of, rows, v):
        return jnp.dot(pick(row_of, rows, G * src), v, preferred_element_type=F32).astype(BF)

    t_rows, q_rows = G * C * th, G * C * qh
    moved_t = move(train_row, t_rows, got[:, :width])
    moved_q = jnp.concatenate(
        [move(query_row(h), q_rows, got[:, width:]) for h in range(2)], 1
    )
    block = jnp.concatenate([moved_t, moved_q], 0)
    block, g0, a0, g1, a1 = lax.optimization_barrier((block, g0, a0, g1, a1))
    full = spread(block, "x", X).reshape(X * (t_rows + q_rows), width)

    inverse = 1.0 / (eigenvalues + damping)

    def wanted(c):
        h, rest = c // d_tile, c % d_tile
        return (rest // d_part) * d_block + h * (L * d_part) + low * d_part + rest % d_part

    sel_r = lax.broadcasted_iota(jnp.int32, (d_all, H * d_tile), 0)
    sel_c = lax.broadcasted_iota(jnp.int32, (d_all, H * d_tile), 1)
    sel = (wanted(sel_c) == sel_r).astype(BF)
    inv_high, inv_low = high_low(inverse)
    chosen = jnp.dot(jnp.concatenate([inv_high, inv_low], 0), sel, preferred_element_type=F32).astype(BF)
    chosen = chosen.reshape(2, f_own, H, d_tile).transpose(2, 1, 0, 3).reshape(H, f_own, 2 * d_tile)
    inv = exchange(chosen, "zh").reshape(f_tile, 2 * d_tile)

    tt, tq = G * th, G * qh
    wt, wq = X // L * tt, X // L * tq
    parts = local_call(
        functools.partial(rotate_kernel, X=X, H=H, L=L, tt=tt, tq=tq, gs=gs, f_own=f_own),
        jax.ShapeDtypeStruct((H * L, f_own + 16 * L + 16, wt + 2 * wq), BF),
        full, g0, g1, a0, a1,
    )
    parts, inv = lax.optimization_barrier((parts, inv))
    parts = lax.all_to_all(parts, ("zh", "zl"), 0, 0, tiled=True)
    g_out, a_out = local_call(
        functools.partial(combine_kernel, n=H * L, f_own=f_own, L=L, wt=wt, wq=wq, d_part=d_part),
        (jax.ShapeDtypeStruct((H * L, f_own, wt + wq), BF), jax.ShapeDtypeStruct((Y * X, 16, L * wt), BF)),
        parts,
    )
    a_all = lax.all_to_all(a_out, ("y", "x"), 0, 0, tiled=True).reshape(Y * X * 16, L * wt)
    a_other = swap(a_all, "c")
    g_all = lax.all_to_all(g_out, ("zh", "zl"), 0, 0, tiled=True)
    g_other = swap(g_all, "c")
    scores = local_call(
        functools.partial(score_kernel, Y=Y, H=H, L=L, wt=wt, wq=wq, d_part=d_part, group=H * qh),
        jax.ShapeDtypeStruct((Y, L * wt), F32),
        a_all, a_other, g_all, g_other, inv,
    )
    n_out = Y * X * H * L
    scores = scores.T.reshape(n_out, scores.shape[1] // n_out * Y)
    mine = lax.all_to_all(scores, ("x", "y", "zh", "zl"), 0, 0, tiled=True).sum(0)
    return mine.reshape(-1, Y)


def factored(mesh):
    devices = mesh.devices
    ex, blk = devices.shape
    xs, cores = 4, 2
    zh = 4
    return Mesh(
        devices.reshape(ex // (xs * zh), xs, zh, blk // cores, cores), ("y", "x", "zh", "zl", "c")
    )


def solution(mesh):
    ex, blk = ("y", "x", "zh"), ("zl", "c")
    placed = (
        P(ex, blk),
        P(ex, blk),
        P(ex),
        P(ex, blk),
        P(ex, blk),
        P(blk, ex),
        P(blk, ex),
        P(ex, None),
    )
    return jax.shard_map(
        per_device, mesh=factored(mesh), in_specs=placed, out_specs=P(ex + blk, None), check_vma=False
    )
```

```python
import functools

import jax
import jax.numpy as jnp
from jax import lax
from jax.experimental import pallas as pl
from jax.experimental.pallas import tpu as pltpu
from jax.sharding import Mesh, PartitionSpec as P

damping = 0.1

BF = jnp.bfloat16
F32 = jnp.float32


def high_low(v):
    high = v.astype(BF)
    return high, (v - high.astype(F32)).astype(BF)


def swap(v, axis):
    return lax.ppermute(v, axis, [(0, 1), (1, 0)])


def exchange(pieces, axis):
    n = lax.axis_size(axis)
    me = lax.axis_index(axis)
    received = [lax.dynamic_index_in_dim(pieces, me, 0, keepdims=False)]
    for step in range(1, n):
        out = lax.dynamic_index_in_dim(pieces, (me + step) % n, 0, keepdims=False)
        received.append(lax.ppermute(out, axis, [(i, (i + step) % n) for i in range(n)]))
    return received


def iota(shape, dim):
    return lax.broadcasted_iota(jnp.int32, shape, dim)


def matmul(a, b):
    return jnp.dot(a, b, preferred_element_type=F32)


def lanes(v, shift, start, stop):
    n = v.shape[1]
    if shift % n:
        v = pltpu.roll(v, shift % n, 1)
    c = iota(v.shape, 1)
    return jnp.where((c >= start) & (c < stop), v, 0.0)


LANES = 128


def message_kernel(tg_ref, ta_ref, mask_ref, qg_ref, qa_ref, mine_ref, theirs_ref, *, H, L, C):
    core = lax.axis_index("c")
    nt, nq = tg_ref.shape[0], qg_ref.shape[0]
    th, per = nt // C, nt // (L * C)
    r, c = iota((2 * nt, nt), 0), iota((2 * nt, nt), 1)
    first = r < th
    owner = jnp.where(first, core, 1 - core)
    k = r % th
    token = (k // per) * (C * per) + owner * per + k % per
    used = first | (r >= 2 * nt - th)
    pick = (used & (token == c)).astype(F32)
    masked = (pick * mask_ref[...].astype(F32)).astype(BF)
    pick = pick.astype(BF)
    r, c = iota((2 * nt, nq), 0), iota((2 * nt, nq), 1)
    first = r < th
    owner = jnp.where(first, core, 1 - core)
    used = first | (r >= 2 * nt - th)
    pick_q = (used & (owner * (nq // C) + (r % th) // 2 == c)).astype(BF)
    tg, ta = matmul(masked, tg_ref[...]), matmul(pick, ta_ref[...])
    qg, qa = matmul(pick_q, qg_ref[...]), matmul(pick_q, qa_ref[...])
    gs = tg.shape[1] // H
    wide = 3 * LANES
    out = []
    for h in range(H):
        low_half = iota((2 * nt, wide), 0) % 2 == 0
        q = qg[:, h * gs:(h + 1) * gs]
        q_high = jnp.concatenate([q[:, wide:], jnp.zeros((2 * nt, 2 * wide - gs), F32)], 1)
        q = jnp.where(low_half, q[:, :wide], q_high)
        low_half = low_half[:, :LANES]
        a_tile, rest = qa[:, h * LANES:(h + 1) * LANES], qa[:, H * LANES:]
        at = 32 * h
        b_tile = lanes(ta[:, H * LANES:], -at, 0, 32) + jnp.where(
            low_half,
            lanes(a_tile, 32, 32, 96) + lanes(rest, 96 - at, 96, 112),
            lanes(a_tile, -32, 32, 96) + lanes(rest, 80 - at, 96, 112),
        )
        out.append(
            jnp.concatenate([tg[:, h * gs:(h + 1) * gs], ta[:, h * LANES:(h + 1) * LANES], b_tile, q], 1)
        )
    mine_ref[...] = jnp.concatenate([v[:nt] for v in out], 0).astype(BF)
    theirs_ref[...] = jnp.concatenate([v[nt:] for v in out], 0).astype(BF)


def shuffle_kernel(got_ref, out_ref, *, G, th, qh, gs):
    src = 2 * th
    n = G * src
    r, c = iota((n, n), 0), iota((n, n), 1)
    rest = r % (G * th)
    pick = (c == (rest // th) * src + (r // (G * th)) * th + rest % th).astype(BF)
    qn = 2 * G * qh
    r, c = iota((qn, n), 0), iota((qn, n), 1)
    rest = r % (G * qh)
    row = (rest // qh) * src + ((r // (G * qh)) * qh + rest % qh) * 2
    picks = [(c == row + half).astype(BF) for half in range(2)]
    width = gs + LANES
    got = got_ref[...]
    train = matmul(pick, got[:, :width + LANES])
    wide = 3 * LANES
    q_grads = jnp.concatenate(
        [matmul(picks[0], got[:, width + LANES:]), matmul(picks[1], got[:, width + LANES:width + LANES + gs - wide])], 1
    )
    v0, v1 = (matmul(p, got[:, width:width + LANES]) for p in picks)
    q_a = lanes(v0, -32, 0, 64) + lanes(v1, 32, 64, 128)
    q_b = lanes(v0, 32, 0, 16) + lanes(v1, 48, 16, 32)
    body = jnp.concatenate([train[:, :width], jnp.concatenate([q_grads, q_a], 1)], 0).astype(BF)
    tail = jnp.concatenate([train[:, width:], q_b], 0)
    rows = tail.shape[0] // 4
    packed = sum(lanes(tail[g * rows:(g + 1) * rows], 32 * g, 32 * g, 32 * g + 32) for g in range(4)).astype(BF)
    tiles = width // LANES
    per = rows // tiles
    packed = jnp.concatenate([packed[k * per:(k + 1) * per] for k in range(tiles)], 1)
    for x in range(out_ref.shape[0]):
        out_ref[x, :n + qn] = body
        out_ref[x, n + qn:] = packed


def rotate_kernel(full_ref, own_ref, other_ref, out_ref, *, X, H, L, tt, tq, gs, f_own):
    me = lax.axis_index("zh")
    per = 2 * (tt + tq)
    inner = X // L
    wt, wq = inner * tt, inner * tq
    tiles = gs // LANES + 1
    group = per // 4
    fine = group // tiles
    grads = [jnp.concatenate([b[s, :f_own] for s in range(H)], 0) for b in (own_ref, other_ref)]
    acts = [jnp.concatenate([b[s, f_own:, :2 * LANES] for s in range(H)], 0) for b in (own_ref, other_ref)]
    for l in range(L):
        blocks = []
        for x in range(inner):
            at = l * inner + x
            packed = jnp.concatenate(
                [full_ref[at, per:, k * LANES:(k + 1) * LANES].astype(F32) for k in range(tiles)], 0
            )
            tail = jnp.concatenate([lanes(packed, -32 * g, 0, 32) for g in range(4)], 0).astype(BF)
            blocks.append((full_ref.at[at], tail))
        g = a = 0.0
        for s in range(2):
            spans = [(b, t, s * tt, tt) for b, t in blocks] + [(b, t, 2 * tt + s * tq, tq) for b, t in blocks]
            tokens = jnp.concatenate([b[p:p + m, :gs] for b, _, p, m in spans], 0)
            inputs = jnp.concatenate(
                [jnp.concatenate([b[p:p + m, gs:], t[p:p + m]], 1) for b, t, p, m in spans], 0
            )
            g += lax.dot_general(grads[s], tokens, (((1,), (1,)), ((), ())), preferred_element_type=F32)
            a += lax.dot_general(acts[s], inputs, (((1,), (1,)), ((), ())), preferred_element_type=F32)
        g_high, g_low = high_low(g[:, wt:])
        g_train = g[:, :wt].astype(BF)
        a_high, a_low = high_low(a)
        for s in range(H):
            h = lax.rem(me - s + H, H)
            m = h * L + l
            out_ref[m, :f_own, :wt] = g_train[s * f_own:(s + 1) * f_own]
            out_ref[m, :f_own, wt:wt + wq] = g_high[s * f_own:(s + 1) * f_own]
            out_ref[m, :f_own, wt + wq:] = g_low[s * f_own:(s + 1) * f_own]
            for k in range(L):
                m = h * L + k
                r = slice((s * L + k) * 16, (s * L + k) * 16 + 16)
                at = f_own + 16 * l
                out_ref[m, at:at + 16, :wt] = a_high[r, :wt]
                out_ref[m, at:at + 16, wt:] = a_low[r, :wt]
                at = f_own + 16 * L
                out_ref[m, at:at + 16, l * 2 * wq:l * 2 * wq + wq] = a_high[r, wt:]
                out_ref[m, at:at + 16, l * 2 * wq + wq:(l + 1) * 2 * wq] = a_low[r, wt:]


def combine_kernel(parts_ref, g_ref, a_ref, *, n, f_own, L, wt, wq, d_part):
    total = parts_ref[0].astype(F32)
    for k in range(1, n):
        total += parts_ref[k].astype(F32)
    g_train = total[:f_own, :wt].astype(BF)
    g_query = (total[:f_own, wt:wt + wq] + total[:f_own, wt + wq:]).astype(BF)
    g_ref[:, :wt] = g_train
    g_ref[:, wt:] = g_query
    a_train = [total[f_own + 16 * l:f_own + 16 * l + 16] for l in range(L)]
    a_train = jnp.concatenate([t[:, :wt] + t[:, wt:] for t in a_train], 1)
    last = total[f_own + 16 * L:]
    a_query = jnp.concatenate(
        [last[:, l * 2 * wq:l * 2 * wq + wq] + last[:, l * 2 * wq + wq:(l + 1) * 2 * wq] for l in range(L)], 1
    ).astype(BF)
    half = d_part // 2
    r = lax.broadcasted_iota(jnp.int32, (16, 16), 0)
    c = lax.broadcasted_iota(jnp.int32, (16, 16), 1)
    inside = (r >= d_part) & (r < d_part + half)
    sides = [
        jnp.dot((inside & (c == r - d_part + k * half)).astype(BF), a_query, preferred_element_type=F32)
        for k in range(2)
    ]
    packed = (a_train + jnp.concatenate(sides, 1)).astype(BF)
    for k in range(a_ref.shape[0]):
        a_ref[k] = packed


def score_kernel(
    a_ref, ao_ref, g0_ref, g1_ref, g2_ref, g3_ref, go_ref, inv_ref, out_ref, *, Y, L, wt, wq, d_part, group
):
    low = lax.axis_index("zl")
    pieces = (g0_ref, g1_ref, g2_ref, g3_ref)
    half = d_part // 2
    n = a_ref.shape[0]
    r, c = iota((n, n), 0), iota((n, n), 1)
    j = r % 16
    base = r - j + d_part
    unpack = [
        ((j >= k * half) & (j < (k + 1) * half) & (c == base + j - k * half)).astype(BF) for k in range(2)
    ]

    def query_acts(ref):
        width = ref.shape[1] // 2
        return (matmul(unpack[0], ref[:, :width]) + matmul(unpack[1], ref[:, width:])).astype(BF)

    def chunks(own, other):
        return jnp.concatenate([jnp.where(low == 0, own, other), jnp.where(low == 0, other, own)], 1)

    def grads(cols):
        return chunks(*(jnp.concatenate([p[k, :, cols] for p in pieces], 0).astype(F32) for k in range(L)))

    f_own = go_ref.shape[1]
    theirs = [jnp.concatenate([go_ref[s * L + k] for s in range(len(pieces))], 0).astype(F32) for k in range(L)]
    qa = jnp.concatenate([query_acts(a_ref), query_acts(ao_ref)], 1)
    qg = jnp.concatenate([grads(slice(wt, wt + wq)), chunks(*theirs)], 1).astype(BF)
    g_train = grads(slice(0, wt))
    d_tile = inv_ref.shape[1] // 2
    r, c = iota((d_tile, n), 0), iota((d_tile, n), 1)
    place = (c == (r // d_part) * 16 + r % d_part).astype(BF)
    inv = matmul(inv_ref[:, :d_tile], place) + matmul(inv_ref[:, d_tile:], place)
    owner = (iota(qg.shape, 1) // group) % Y
    acts = a_ref[...]
    for q in range(Y):
        raw = lax.dot_general(
            jnp.where(owner == q, qg, jnp.zeros_like(qg)), qa, (((1,), (1,)), ((), ())), preferred_element_type=F32
        )
        mixed = matmul((raw * inv).astype(BF), acts)
        out_ref[q:q + 1, :] = jnp.sum(mixed * g_train, axis=0, keepdims=True)


def local_call(kernel, shapes, *args):
    return pl.pallas_call(
        kernel,
        out_shape=shapes,
        in_specs=[pl.BlockSpec(memory_space=pltpu.VMEM)] * len(args),
        out_specs=jax.tree.map(lambda _: pl.BlockSpec(memory_space=pltpu.VMEM), shapes),
        compiler_params=pltpu.CompilerParams(vmem_limit_bytes=40 * 2**20),
    )(*args)


def per_device(
    train_grads, train_acts, train_mask, query_grads, query_acts, grad_basis, act_basis, eigenvalues
):
    Y, X, H, L, C = (lax.axis_size(a) for a in ("y", "x", "zh", "zl", "c"))
    low = lax.axis_index("zl")
    gk, f_own = grad_basis.shape
    ak, d_own = act_basis.shape
    gs, as_ = gk // H, ak // H
    nt, nq = train_grads.shape[0], query_grads.shape[0]
    th, qh = nt // C, nq // C
    d_all = eigenvalues.shape[1]
    f_tile, d_block = f_own * H, d_own * H
    d_part = d_block // (H * L)
    d_tile = d_part * X * Y

    mine, theirs = local_call(
        functools.partial(message_kernel, H=H, L=L, C=C),
        [jax.ShapeDtypeStruct((H * nt, 2 * gs), BF)] * 2,
        train_grads, train_acts, train_mask.reshape(1, nt), query_grads, query_acts,
    )
    message = mine + swap(theirs, "c")
    message = jnp.broadcast_to(message.reshape(1, H, nt, 2 * gs), (Y, H, nt, 2 * gs)).reshape(Y * H, nt, 2 * gs)
    message, grad_basis, act_basis, eigenvalues = lax.optimization_barrier(
        (message, grad_basis, act_basis, eigenvalues)
    )
    got = lax.all_to_all(message, ("y", "zh"), 0, 0, tiled=True)

    gb = grad_basis.T.reshape(f_own, H, gs).transpose(1, 0, 2)
    ab = act_basis.T
    main = ab[:, :H * LANES].reshape(d_own, H, LANES)
    rest = ab[:, H * LANES:].reshape(d_own, H, as_ - LANES)
    ab = jnp.concatenate([main, rest], 2).transpose(1, 0, 2).reshape(H, L, d_part, as_)
    ab = jnp.pad(ab, ((0, 0), (0, 0), (0, 16 - d_part), (0, gs - as_))).reshape(H, L * 16, gs)
    pieces = jnp.concatenate([gb, ab], 1)

    inverse = 1.0 / (eigenvalues + damping)

    def wanted(c):
        h, rest = c // d_tile, c % d_tile
        return (rest // d_part) * d_block + h * (L * d_part) + low * d_part + rest % d_part

    sel = (wanted(iota((d_all, H * d_tile), 1)) == iota((d_all, H * d_tile), 0)).astype(BF)
    inv_high, inv_low = high_low(inverse)
    chosen = jnp.dot(jnp.concatenate([inv_high, inv_low], 0), sel, preferred_element_type=F32).astype(BF)
    chosen = chosen.reshape(2, f_own, H, d_tile).transpose(2, 1, 0, 3).reshape(H, f_own, 2 * d_tile)
    got, pieces, chosen = lax.optimization_barrier((got, pieces, chosen))

    G = Y * H
    block = local_call(
        functools.partial(shuffle_kernel, G=G, th=th, qh=qh, gs=gs),
        jax.ShapeDtypeStruct((X, G * C * (th + qh) * 25 // 24, gs + LANES), BF),
        got.reshape(G * nt, 2 * gs),
    )
    full = lax.all_to_all(block, "x", 0, 0, tiled=True)
    own = jnp.stack(exchange(pieces, "zh"))
    other = swap(own, "c")

    tt, tq = G * th, G * qh
    wt, wq = X // L * tt, X // L * tq
    parts = local_call(
        functools.partial(rotate_kernel, X=X, H=H, L=L, tt=tt, tq=tq, gs=gs, f_own=f_own),
        jax.ShapeDtypeStruct((H * L, f_own + 16 * L + 16, wt + 2 * wq), BF),
        full, own, other,
    )
    parts, chosen = lax.optimization_barrier((parts, chosen))
    parts = lax.all_to_all(parts, ("zh", "zl"), 0, 0, tiled=True)
    inv = jnp.concatenate(exchange(chosen, "zh"), 0)
    parts, inv = lax.optimization_barrier((parts, inv))
    g_out, a_out = local_call(
        functools.partial(combine_kernel, n=H * L, f_own=f_own, L=L, wt=wt, wq=wq, d_part=d_part),
        (jax.ShapeDtypeStruct((f_own, wt + wq), BF), jax.ShapeDtypeStruct((Y * X, 16, L * wt), BF)),
        parts,
    )
    a_all = lax.all_to_all(a_out, ("y", "x"), 0, 0, tiled=True).reshape(Y * X * 16, L * wt)
    a_other = swap(a_all, "c")
    pair = jnp.stack([g_out, swap(g_out, "zl")])
    g_all = [pair] + [
        lax.ppermute(pair, "zh", [(i, (i + step) % H) for i in range(H)]) for step in range(1, H)
    ]
    g_other = swap(jnp.concatenate([p[:, :, wt:] for p in g_all], 0), "c")
    scores = local_call(
        functools.partial(score_kernel, Y=Y, L=L, wt=wt, wq=wq, d_part=d_part, group=H * qh),
        jax.ShapeDtypeStruct((Y, L * wt), F32),
        a_all, a_other, *g_all, g_other, inv,
    )
    n_out = Y * X * H * L
    scores = scores.T.reshape(n_out, scores.shape[1] // n_out * Y)
    mine = lax.all_to_all(scores, ("x", "y", "zh", "zl"), 0, 0, tiled=True).sum(0)
    return mine.reshape(-1, Y)


def factored(mesh):
    devices = mesh.devices
    ex, blk = devices.shape
    xs, cores = 4, 2
    zh = 4
    return Mesh(
        devices.reshape(ex // (xs * zh), xs, zh, blk // cores, cores), ("y", "x", "zh", "zl", "c")
    )


def solution(mesh):
    ex, blk = ("y", "x", "zh"), ("zl", "c")
    placed = (
        P(ex, blk),
        P(ex, blk),
        P(ex),
        P(ex, blk),
        P(ex, blk),
        P(blk, ex),
        P(blk, ex),
        P(ex, None),
    )
    return jax.shard_map(
        per_device, mesh=factored(mesh), in_specs=placed, out_specs=P(ex + blk, None), check_vma=False
    )
```

```python
import functools

import jax
import jax.numpy as jnp
from jax import lax
from jax.experimental import pallas as pl
from jax.experimental.pallas import tpu as pltpu
from jax.sharding import Mesh, PartitionSpec as P

damping = 0.1

BF = jnp.bfloat16
F32 = jnp.float32


def high_low(v):
    high = v.astype(BF)
    return high, (v - high.astype(F32)).astype(BF)


def swap(v, axis):
    return lax.ppermute(v, axis, [(0, 1), (1, 0)])


def exchange(pieces, axis, step):
    n = lax.axis_size(axis)
    out = lax.dynamic_index_in_dim(pieces, (lax.axis_index(axis) + step) % n, 0, keepdims=False)
    return out if step == 0 else lax.ppermute(out, axis, [(i, (i + step) % n) for i in range(n)])


def iota(shape, dim):
    return lax.broadcasted_iota(jnp.int32, shape, dim)


def matmul(a, b):
    return jnp.dot(a, b, preferred_element_type=F32)


def lanes(v, shift, start, stop):
    n = v.shape[1]
    if shift % n:
        v = pltpu.roll(v, shift % n, 1)
    c = iota(v.shape, 1)
    return jnp.where((c >= start) & (c < stop), v, 0.0)


LANES = 128


def message_kernel(tg_ref, ta_ref, mask_ref, qg_ref, qa_ref, mine_ref, theirs_ref, *, H, L, C):
    core = lax.axis_index("c")
    nt, nq = tg_ref.shape[0], qg_ref.shape[0]
    th, per = nt // C, nt // (L * C)
    r, c = iota((2 * nt, nt), 0), iota((2 * nt, nt), 1)
    first = r < th
    owner = jnp.where(first, core, 1 - core)
    k = r % th
    token = (k // per) * (C * per) + owner * per + k % per
    used = first | (r >= 2 * nt - th)
    pick = (used & (token == c)).astype(F32)
    masked = (pick * mask_ref[...].astype(F32)).astype(BF)
    pick = pick.astype(BF)
    r, c = iota((2 * nt, nq), 0), iota((2 * nt, nq), 1)
    first = r < th
    owner = jnp.where(first, core, 1 - core)
    used = first | (r >= 2 * nt - th)
    pick_q = (used & (owner * (nq // C) + (r % th) // 2 == c)).astype(BF)
    tg, ta = matmul(masked, tg_ref[...]), matmul(pick, ta_ref[...])
    qg, qa = matmul(pick_q, qg_ref[...]), matmul(pick_q, qa_ref[...])
    gs = tg.shape[1] // H
    wide = 3 * LANES
    out = []
    for h in range(H):
        low_half = iota((2 * nt, wide), 0) % 2 == 0
        q = qg[:, h * gs:(h + 1) * gs]
        q_high = jnp.concatenate([q[:, wide:], jnp.zeros((2 * nt, 2 * wide - gs), F32)], 1)
        q = jnp.where(low_half, q[:, :wide], q_high)
        low_half = low_half[:, :LANES]
        a_tile, rest = qa[:, h * LANES:(h + 1) * LANES], qa[:, H * LANES:]
        at = 32 * h
        b_tile = lanes(ta[:, H * LANES:], -at, 0, 32) + jnp.where(
            low_half,
            lanes(a_tile, 32, 32, 96) + lanes(rest, 96 - at, 96, 112),
            lanes(a_tile, -32, 32, 96) + lanes(rest, 80 - at, 96, 112),
        )
        out.append(
            jnp.concatenate([tg[:, h * gs:(h + 1) * gs], ta[:, h * LANES:(h + 1) * LANES], b_tile, q], 1)
        )
    mine_ref[...] = jnp.concatenate([v[:nt] for v in out], 0).astype(BF)
    theirs_ref[...] = jnp.concatenate([v[nt:] for v in out], 0).astype(BF)


def shuffle_kernel(got_ref, out_ref, *, G, th, qh, gs):
    src = 2 * th
    n = G * src
    r, c = iota((n, n), 0), iota((n, n), 1)
    rest = r % (G * th)
    pick = (c == (rest // th) * src + (r // (G * th)) * th + rest % th).astype(BF)
    qn = 2 * G * qh
    r, c = iota((qn, n), 0), iota((qn, n), 1)
    rest = r % (G * qh)
    row = (rest // qh) * src + ((r // (G * qh)) * qh + rest % qh) * 2
    picks = [(c == row + half).astype(BF) for half in range(2)]
    width = gs + LANES
    got = got_ref[...]
    train = matmul(pick, got[:, :width + LANES])
    wide = 3 * LANES
    q_grads = jnp.concatenate(
        [matmul(picks[0], got[:, width + LANES:]), matmul(picks[1], got[:, width + LANES:width + LANES + gs - wide])], 1
    )
    v0, v1 = (matmul(p, got[:, width:width + LANES]) for p in picks)
    q_a = lanes(v0, -32, 0, 64) + lanes(v1, 32, 64, 128)
    q_b = lanes(v0, 32, 0, 16) + lanes(v1, 48, 16, 32)
    body = jnp.concatenate([train[:, :width], jnp.concatenate([q_grads, q_a], 1)], 0).astype(BF)
    tail = jnp.concatenate([train[:, width:], q_b], 0)
    rows = tail.shape[0] // 4
    packed = sum(lanes(tail[g * rows:(g + 1) * rows], 32 * g, 32 * g, 32 * g + 32) for g in range(4)).astype(BF)
    packed = jnp.concatenate([packed[k:k + 16] for k in range(0, rows, 16)], 1)
    for x in range(out_ref.shape[0]):
        out_ref[x, :n + qn] = body
        out_ref[x, n + qn:, :packed.shape[1]] = packed


def rotate_kernel(full_ref, own_ref, other_ref, out_ref, *, H, L, tt, tq, gs, f_own, d_part):
    me = lax.axis_index("zh")
    per = 2 * (tt + tq)
    inner = full_ref.shape[0] // L
    wt, wq = inner * tt, inner * tq
    group = per // 4
    grads = [jnp.concatenate([b[s, :f_own, :gs] for s in range(H)], 0) for b in (own_ref, other_ref)]
    acts = [
        jnp.concatenate([b[s, f_own:, k * 2 * LANES:(k + 1) * 2 * LANES] for s in range(H) for k in range(L)], 0)
        for b in (own_ref, other_ref)
    ]
    r, c = iota((H * L * 32, H * L * 16), 0), iota((H * L * 32, H * L * 16), 1)
    repeat = ((r % 32 < (L + 1) * d_part) & (c == (r // 32) * 16 + (r % 32) % d_part)).astype(BF)
    acts = [matmul(repeat, v).astype(BF) for v in acts]
    a_parts = []
    for l in range(L):
        blocks = []
        for x in range(inner):
            at = l * inner + x
            packed = jnp.concatenate(
                [full_ref[at, per:, k * LANES:(k + 1) * LANES].astype(F32) for k in range(group // 16)], 0
            )
            tail = jnp.concatenate([lanes(packed, -32 * g, 0, 32) for g in range(4)], 0).astype(BF)
            blocks.append((full_ref.at[at], tail))
        g = a = 0.0
        for s in range(2):
            spans = [(b, t, s * tt, tt) for b, t in blocks] + [(b, t, 2 * tt + s * tq, tq) for b, t in blocks]
            tokens = jnp.concatenate([b[p:p + m, :gs] for b, _, p, m in spans], 0)
            inputs = jnp.concatenate(
                [jnp.concatenate([b[p:p + m, gs:], t[p:p + m]], 1) for b, t, p, m in spans], 0
            )
            g += lax.dot_general(grads[s], tokens, (((1,), (1,)), ((), ())), preferred_element_type=F32)
            a += lax.dot_general(acts[s], inputs, (((1,), (1,)), ((), ())), preferred_element_type=F32)
        a_parts.append(a)
        g_high, g_low = high_low(g[:, wt:])
        g_train = g[:, :wt].astype(BF)
        for s in range(H):
            m = lax.rem(me - s + H, H) * L + l
            out_ref[m, :f_own, :wt] = g_train[s * f_own:(s + 1) * f_own]
            out_ref[m, :f_own, wt:wt + wq] = g_high[s * f_own:(s + 1) * f_own]
            out_ref[m, :f_own, wt + wq:] = g_low[s * f_own:(s + 1) * f_own]
    merged = jnp.concatenate([a[:, wt:] for a in a_parts], 1)
    kind = (iota(merged.shape, 0) % 32) // d_part
    for l in range(L):
        merged = jnp.where(kind == l, a_parts[l][:, :wt], merged)
    a_high, a_low = high_low(merged)
    for s in range(H):
        for k in range(L):
            m = lax.rem(me - s + H, H) * L + k
            r = slice((s * L + k) * 32, (s * L + k + 1) * 32)
            out_ref[m, f_own:, :wt] = a_high[r]
            out_ref[m, f_own:, wt:] = a_low[r]


def combine_kernel(parts_ref, g_ref, a_ref, *, n, f_own, L, wt, wq, d_part):
    total = parts_ref[0].astype(F32)
    for k in range(1, n):
        total += parts_ref[k].astype(F32)
    g_train = total[:f_own, :wt].astype(BF)
    g_query = (total[:f_own, wt:wt + wq] + total[:f_own, wt + wq:]).astype(BF)
    g_ref[:, :wt] = g_train
    g_ref[:, wt:] = g_query
    act = total[f_own:, :wt] + total[f_own:, wt:]
    inside = iota((16, wt), 0) < d_part
    kinds = [jnp.where(inside, (pltpu.roll(act, 32 - k * d_part, 0) if k else act)[:16], 0.0) for k in range(L + 1)]
    a_train = jnp.concatenate(kinds[:L], 1)
    a_query = kinds[L].astype(BF)
    half = d_part // 2
    r = lax.broadcasted_iota(jnp.int32, (16, 16), 0)
    c = lax.broadcasted_iota(jnp.int32, (16, 16), 1)
    inside = (r >= d_part) & (r < d_part + half)
    sides = [
        jnp.dot((inside & (c == r - d_part + k * half)).astype(BF), a_query, preferred_element_type=F32)
        for k in range(2)
    ]
    packed = (a_train + jnp.concatenate(sides, 1)).astype(BF)
    for k in range(a_ref.shape[0]):
        a_ref[k] = packed


def score_kernel(
    a_ref, ao_ref, g_ref, go_ref, inv_ref, invo_ref, out_ref, inv_acc, *, Y, YL, L, wt, wq, d_part, group, n_d
):
    H, f_own, d_tile = g_ref.shape[0], g_ref.shape[2], n_d
    half = d_part // 2
    n = a_ref.shape[0]
    r, c = iota((n, n), 0), iota((n, n), 1)
    j = r % 16
    base = r - j + d_part
    unpack = [
        ((j >= k * half) & (j < (k + 1) * half) & (c == base + j - k * half)).astype(BF) for k in range(2)
    ]

    def query_acts(ref):
        width = ref.shape[1] // 2
        return (matmul(unpack[0], ref[:, :width]) + matmul(unpack[1], ref[:, width:])).astype(BF)

    def grads(ref, cols):
        return jnp.concatenate(
            [jnp.concatenate([ref[h, k, :, cols] for h in range(H)], 0) for k in range(L)], 1
        )

    qa = jnp.concatenate([query_acts(a_ref), query_acts(ao_ref)], 1)
    qg = jnp.concatenate([grads(g_ref, slice(wt, wt + wq)), grads(go_ref, slice(0, wq))], 1)
    g_train = grads(g_ref, slice(0, wt)).astype(F32)
    r, c = iota((d_tile, n), 0), iota((d_tile, n), 1)
    place = (c == (r // d_part) * 16 + r % d_part).astype(BF)
    me = lax.axis_index("zh")
    for s in range(H):
        rows = pl.ds(pl.multiple_of(lax.rem(me - s + H, H) * f_own, f_own), f_own)
        inv_acc[rows, :] = matmul(inv_ref[s, :f_own, -d_tile:], place) + matmul(invo_ref[s, :f_own, -d_tile:], place)
    inv = inv_acc[...]
    col = iota(qg.shape, 1)
    owner = (col // group) % (Y // YL) * YL + (col // (group * (Y // YL))) % YL
    acts = a_ref[...]
    for q in range(Y):
        raw = lax.dot_general(
            jnp.where(owner == q, qg, jnp.zeros_like(qg)), qa, (((1,), (1,)), ((), ())), preferred_element_type=F32
        )
        mixed = matmul((raw * inv).astype(BF), acts)
        out_ref[q:q + 1, :] = jnp.sum(mixed * g_train, axis=0, keepdims=True)


def staged_call(kernel, shapes, *args):
    whole = lambda v: pl.BlockSpec(v.shape, lambda i: (0,) * len(v.shape))
    return pl.pallas_call(
        kernel,
        grid=(1,),
        out_shape=shapes,
        in_specs=[whole(v) for v in args],
        out_specs=[whole(v) for v in shapes],
    )(*args)


def local_call(kernel, shapes, *args, scratch=()):
    return pl.pallas_call(
        kernel,
        out_shape=shapes,
        in_specs=[pl.BlockSpec(memory_space=pltpu.VMEM)] * len(args),
        out_specs=jax.tree.map(lambda _: pl.BlockSpec(memory_space=pltpu.VMEM), shapes),
        scratch_shapes=scratch,
        compiler_params=pltpu.CompilerParams(vmem_limit_bytes=40 * 2**20),
    )(*args)


def per_device(
    train_grads, train_acts, train_mask, query_grads, query_acts, grad_basis, act_basis, eigenvalues
):
    YH, YL, X, H, L, C = (lax.axis_size(a) for a in ("yh", "yl", "x", "zh", "zl", "c"))
    Y = YH * YL
    low = lax.axis_index("zl")
    gk, f_own = grad_basis.shape
    ak, d_own = act_basis.shape
    gs, as_ = gk // H, ak // H
    nt, nq = train_grads.shape[0], query_grads.shape[0]
    th, qh = nt // C, nq // C
    d_all = eigenvalues.shape[1]
    f_tile, d_block = f_own * H, d_own * H
    d_part = d_block // (H * L)
    d_tile = d_part * X * Y

    mine, theirs = staged_call(
        functools.partial(message_kernel, H=H, L=L, C=C),
        [jax.ShapeDtypeStruct((H * nt, 2 * gs), BF)] * 2,
        train_grads, train_acts, train_mask.reshape(1, nt), query_grads, query_acts,
    )
    message = mine + swap(theirs, "c")
    message = jnp.broadcast_to(message.reshape(1, H, nt, 2 * gs), (YH, H, nt, 2 * gs)).reshape(YH * H, nt, 2 * gs)
    message, grad_basis, act_basis, eigenvalues = lax.optimization_barrier(
        (message, grad_basis, act_basis, eigenvalues)
    )
    got = lax.all_to_all(message, ("yh", "zh"), 0, 0, tiled=True)

    gb = grad_basis.T.reshape(f_own, H, gs).transpose(1, 0, 2)
    ab = act_basis.T
    main = ab[:, :H * LANES].reshape(d_own, H, LANES)
    rest = ab[:, H * LANES:].reshape(d_own, H, as_ - LANES)
    ab = jnp.concatenate([main, rest], 2).reshape(L, d_part, H, as_).transpose(2, 1, 0, 3)
    ab = jnp.pad(ab, ((0, 0), (0, 16 - d_part), (0, 0), (0, 2 * LANES - as_))).reshape(H, 16, L * 2 * LANES)
    ab = jnp.pad(ab, ((0, 0), (0, 0), (0, gs - L * 2 * LANES)))
    pieces = jnp.concatenate([gb, ab], 1)

    inverse = 1.0 / (eigenvalues + damping)

    def wanted(c):
        h, rest = c // d_tile, c % d_tile
        return (rest // d_part) * d_block + h * (L * d_part) + low * d_part + rest % d_part

    sel = (wanted(iota((d_all, H * d_tile), 1)) == iota((d_all, H * d_tile), 0)).astype(BF)
    inv_high, inv_low = high_low(inverse)
    half = jnp.where(lax.axis_index("c") == 0, inv_high, inv_low)
    chosen = jnp.dot(half, sel, preferred_element_type=F32).astype(BF)
    chosen = chosen.reshape(f_own, H, d_tile).transpose(1, 0, 2)
    pieces = jnp.concatenate([pieces, jnp.pad(chosen, ((0, 0), (0, 16), (0, 0)))], 2)
    got, pieces = lax.optimization_barrier((got, pieces))

    G = YH * H
    block = local_call(
        functools.partial(shuffle_kernel, G=G, th=th, qh=qh, gs=gs),
        jax.ShapeDtypeStruct((X * YL, G * C * (th + qh) + 16, gs + LANES), BF),
        got.reshape(G * nt, 2 * gs),
    )
    full = lax.all_to_all(block, ("x", "yl"), 0, 0, tiled=True)
    own = jnp.stack([exchange(pieces, "zh", k) for k in range(H)])
    other = swap(own, "c")
    full, own, other = lax.optimization_barrier((full, own, other))

    tt, tq = G * th, G * qh
    wt, wq = X // L * YL * tt, X // L * YL * tq
    parts = local_call(
        functools.partial(rotate_kernel, H=H, L=L, tt=tt, tq=tq, gs=gs, f_own=f_own, d_part=d_part),
        jax.ShapeDtypeStruct((H * L, f_own + 32, wt + 2 * wq), BF),
        full, own, other,
    )
    parts = lax.all_to_all(parts, ("zh", "zl"), 0, 0, tiled=True)
    g_out, a_out = local_call(
        functools.partial(combine_kernel, n=H * L, f_own=f_own, L=L, wt=wt, wq=wq, d_part=d_part),
        (jax.ShapeDtypeStruct((f_own, wt + wq), BF), jax.ShapeDtypeStruct((Y * X, 16, L * wt), BF)),
        parts,
    )
    a_all = lax.all_to_all(a_out, ("yh", "yl", "x"), 0, 0, tiled=True).reshape(Y * X * 16, L * wt)
    g_all = lax.all_gather(lax.all_gather(g_out, "zl"), "zh")
    a_all, g_all = lax.optimization_barrier((a_all, g_all))
    a_other = swap(a_all, "c")
    g_other = swap(g_all[..., wt:], "c")
    scores = local_call(
        functools.partial(
            score_kernel, Y=Y, YL=YL, L=L, wt=wt, wq=wq, d_part=d_part, group=H * qh, n_d=d_tile
        ),
        jax.ShapeDtypeStruct((Y, L * wt), F32),
        a_all, a_other, g_all, g_other, own, other,
        scratch=[pltpu.VMEM((f_tile, Y * X * 16), F32)],
    )
    n_out = Y * X * H * L
    scores = scores.T.reshape(n_out, scores.shape[1] // n_out * Y)
    mine = lax.all_to_all(scores, ("x", "yl", "yh", "zh", "zl"), 0, 0, tiled=True).sum(0)
    return mine.reshape(-1, Y)


def factored(mesh):
    devices = mesh.devices
    ex, blk = devices.shape
    yl, xs, zh, cores = 2, 4, 4, 2
    return Mesh(
        devices.reshape(ex // (yl * xs * zh), yl, xs, zh, blk // cores, cores), ("yh", "yl", "x", "zh", "zl", "c")
    )


def solution(mesh):
    ex, blk = ("yh", "yl", "x", "zh"), ("zl", "c")
    placed = (
        P(ex, blk),
        P(ex, blk),
        P(ex),
        P(ex, blk),
        P(ex, blk),
        P(blk, ex),
        P(blk, ex),
        P(ex, None),
    )
    return jax.shard_map(
        per_device, mesh=factored(mesh), in_specs=placed, out_specs=P(ex + blk, None), check_vma=False
    )
```

```python
import functools

import jax
import jax.numpy as jnp
from jax import lax
from jax.experimental import pallas as pl
from jax.experimental.pallas import tpu as pltpu
from jax.sharding import Mesh, PartitionSpec as P

damping = 0.1

BF = jnp.bfloat16
F32 = jnp.float32


def high_low(v):
    high = v.astype(BF)
    return high, (v - high.astype(F32)).astype(BF)


def swap(v, axis):
    return lax.ppermute(v, axis, [(0, 1), (1, 0)])


def exchange(pieces, axis, step):
    n = lax.axis_size(axis)
    out = lax.dynamic_index_in_dim(pieces, (lax.axis_index(axis) + step) % n, 0, keepdims=False)
    return out if step == 0 else lax.ppermute(out, axis, [(i, (i + step) % n) for i in range(n)])


def iota(shape, dim):
    return lax.broadcasted_iota(jnp.int32, shape, dim)


def matmul(a, b):
    return jnp.dot(a, b, preferred_element_type=F32)


def lanes(v, shift, start, stop):
    n = v.shape[1]
    if shift % n:
        v = pltpu.roll(v, shift % n, 1)
    c = iota(v.shape, 1)
    return jnp.where((c >= start) & (c < stop), v, 0.0)


LANES = 128


def message_kernel(tg_ref, ta_ref, mask_ref, qg_ref, qa_ref, out_ref, *, H, L, C):
    nt, nq = tg_ref.shape[0], qg_ref.shape[0]
    th, per = nt // C, nt // (L * C)
    rows = 2 * th * C

    def pick(n, row_of, upper):
        r, c = iota((rows, n), 0), iota((rows, n), 1)
        owner, k = r // (2 * th), r % th
        return ((r // th) % 2 == upper) & (row_of(owner, k) == c)

    def train(owner, k):
        return (k // per) * (C * per) + owner * per + k % per

    def query(owner, k):
        return owner * (nq // C) + k // 2

    masked = (pick(nt, train, 0).astype(F32) * mask_ref[...].astype(F32)).astype(BF)
    pick_q = pick(nq, query, 1).astype(BF)
    tg, ta = matmul(masked, tg_ref[...]), matmul(pick(nt, train, 1).astype(BF), ta_ref[...])
    qg, qa = matmul(pick_q, qg_ref[...]), matmul(pick_q, qa_ref[...])
    gs = tg.shape[1] // H
    wide = 3 * LANES
    low_half = iota((rows, wide), 0) % 2 == 0
    for h in range(H):
        q = qg[:, h * gs:(h + 1) * gs]
        q_high = jnp.concatenate([q[:, wide:], jnp.zeros((rows, 2 * wide - gs), F32)], 1)
        q = jnp.where(low_half, q[:, :wide], q_high)
        a_tile, rest = qa[:, h * LANES:(h + 1) * LANES], qa[:, H * LANES:]
        at = 32 * h
        b_tile = lanes(ta[:, H * LANES:], -at, 0, 32) + jnp.where(
            low_half[:, :LANES],
            lanes(a_tile, 32, 32, 96) + lanes(rest, 96 - at, 96, 112),
            lanes(a_tile, -32, 32, 96) + lanes(rest, 80 - at, 96, 112),
        )
        v = tg[:, h * gs:(h + 1) * gs] + jnp.concatenate([ta[:, h * LANES:(h + 1) * LANES], b_tile, q], 1)
        v = v.astype(BF)
        for y in range(out_ref.shape[0]):
            out_ref[y, h * rows:(h + 1) * rows] = v


def shuffle_kernel(got_ref, out_ref, *, G, th, qh, gs):
    core = lax.axis_index("c")
    n = got_ref.shape[0]
    each = 2 * th

    def pick(count, per, row_of):
        r, c = iota((count, n), 0), iota((count, n), 1)
        rest = r % (G * per)
        source = (core + r // (G * per)) % 2
        return (c == (rest // per) * (2 * each) + source * each + row_of(rest % per)).astype(BF)

    tn, qn = 2 * G * th, 2 * G * qh
    got = got_ref[...]
    t_grads = matmul(pick(tn, th, lambda k: k), got)
    t_acts = matmul(pick(tn, th, lambda k: th + k), got[:, :2 * LANES])
    q0, q1 = (matmul(pick(qn, qh, lambda k: th + 2 * k + half), got) for half in range(2))
    wide = 3 * LANES
    at = 2 * LANES
    q_grads = jnp.concatenate([q0[:, at:], q1[:, at:at + gs - wide]], 1)
    v0, v1 = q0[:, LANES:at], q1[:, LANES:at]
    q_a = lanes(v0, -32, 0, 64) + lanes(v1, 32, 64, 128)
    q_b = lanes(v0, 32, 0, 16) + lanes(v1, 48, 16, 32)
    body = jnp.concatenate(
        [jnp.concatenate([t_grads, t_acts[:, :LANES]], 1), jnp.concatenate([q_grads, q_a], 1)], 0
    ).astype(BF)
    tail = jnp.concatenate([t_acts[:, LANES:], q_b], 0)
    rows = tail.shape[0] // 4
    packed = sum(lanes(tail[g * rows:(g + 1) * rows], 32 * g, 32 * g, 32 * g + 32) for g in range(4)).astype(BF)
    packed = jnp.concatenate([packed[k:k + 16] for k in range(0, rows, 16)], 1)
    for x in range(out_ref.shape[0]):
        out_ref[x, :tn + qn] = body
        out_ref[x, tn + qn:, :packed.shape[1]] = packed


def total_kernel(parts_ref, out_ref):
    total = jnp.sum(parts_ref[...], axis=0, keepdims=True)
    width = out_ref.shape[1]
    for k in range(out_ref.shape[0]):
        out_ref[k:k + 1, :] = total[:, k * width:(k + 1) * width]


def rotate_kernel(full_ref, own_ref, other_ref, out_ref, *, H, L, tt, tq, gs, f_own, d_part):
    me = lax.axis_index("zh")
    per = 2 * (tt + tq)
    inner = full_ref.shape[0] // L
    wt, wq = inner * tt, inner * tq
    group = per // 4
    grads = [jnp.concatenate([b[s, :f_own, :gs] for s in range(H)], 0) for b in (own_ref, other_ref)]
    r, c = iota((H * L * 16, H * f_own), 0), iota((H * L * 16, H * f_own), 1)
    d = (r // 16) % L * d_part + r % 16
    picks = [((r % 16 < d_part) & (c == r // (16 * L) * f_own + d * 4 + q)).astype(BF) for q in range(4)]
    acts = []
    for b in (own_ref, other_ref):
        last = jnp.concatenate([b[s, :, b.shape[2] - LANES:] for s in range(H)], 0)
        v = [matmul(p, last) for p in picks]
        a_tile = sum(lanes(v[q], 32 * q - 64, 32 * q, 32 * q + 32) for q in range(4))
        b_tile = sum(lanes(v[q], 8 * q - 96, 8 * q, 8 * q + 8) for q in range(4))
        acts.append(jnp.concatenate([a_tile, b_tile], 1).astype(BF))
    r, c = iota((H * L * 32, H * L * 16), 0), iota((H * L * 32, H * L * 16), 1)
    repeat = ((r % 32 < (L + 1) * d_part) & (c == (r // 32) * 16 + (r % 32) % d_part)).astype(BF)
    acts = [matmul(repeat, v).astype(BF) for v in acts]
    a_parts = []
    for l in range(L):
        blocks = []
        for x in range(inner):
            at = l * inner + x
            packed = jnp.concatenate(
                [full_ref[at, per:, k * LANES:(k + 1) * LANES].astype(F32) for k in range(group // 16)], 0
            )
            tail = jnp.concatenate([lanes(packed, -32 * g, 0, 32) for g in range(4)], 0).astype(BF)
            blocks.append((full_ref.at[at], tail))
        g = a = 0.0
        for s in range(2):
            spans = [(b, t, s * tt, tt) for b, t in blocks] + [(b, t, 2 * tt + s * tq, tq) for b, t in blocks]
            tokens = jnp.concatenate([b[p:p + m, :gs] for b, _, p, m in spans], 0)
            inputs = jnp.concatenate(
                [jnp.concatenate([b[p:p + m, gs:], t[p:p + m]], 1) for b, t, p, m in spans], 0
            )
            g += lax.dot_general(grads[s], tokens, (((1,), (1,)), ((), ())), preferred_element_type=F32)
            a += lax.dot_general(acts[s], inputs, (((1,), (1,)), ((), ())), preferred_element_type=F32)
        a_parts.append(a)
        g_high, g_low = high_low(g[:, wt:])
        g_train = g[:, :wt].astype(BF)
        for s in range(H):
            m = lax.rem(me - s + H, H) * L + l
            out_ref[m, :f_own, :wt] = g_train[s * f_own:(s + 1) * f_own]
            out_ref[m, :f_own, wt:wt + wq] = g_high[s * f_own:(s + 1) * f_own]
            out_ref[m, :f_own, wt + wq:] = g_low[s * f_own:(s + 1) * f_own]
    merged = jnp.concatenate([a[:, wt:] for a in a_parts], 1)
    kind = (iota(merged.shape, 0) % 32) // d_part
    for l in range(L):
        merged = jnp.where(kind == l, a_parts[l][:, :wt], merged)
    a_high, a_low = high_low(merged)
    for s in range(H):
        for k in range(L):
            m = lax.rem(me - s + H, H) * L + k
            r = slice((s * L + k) * 32, (s * L + k + 1) * 32)
            out_ref[m, f_own:, :wt] = a_high[r]
            out_ref[m, f_own:, wt:] = a_low[r]


def combine_kernel(parts_ref, g_ref, a_ref, *, n, f_own, L, wt, wq, d_part):
    total = parts_ref[0].astype(F32)
    for k in range(1, n):
        total += parts_ref[k].astype(F32)
    g_train = total[:f_own, :wt].astype(BF)
    g_query = (total[:f_own, wt:wt + wq] + total[:f_own, wt + wq:]).astype(BF)
    g_ref[:, :wt] = g_train
    g_ref[:, wt:] = g_query
    act = total[f_own:, :wt] + total[f_own:, wt:]
    inside = iota((16, wt), 0) < d_part
    kinds = [jnp.where(inside, (pltpu.roll(act, 32 - k * d_part, 0) if k else act)[:16], 0.0) for k in range(L + 1)]
    a_train = jnp.concatenate(kinds[:L], 1)
    a_query = kinds[L].astype(BF)
    half = d_part // 2
    r = lax.broadcasted_iota(jnp.int32, (16, 16), 0)
    c = lax.broadcasted_iota(jnp.int32, (16, 16), 1)
    inside = (r >= d_part) & (r < d_part + half)
    sides = [
        jnp.dot((inside & (c == r - d_part + k * half)).astype(BF), a_query, preferred_element_type=F32)
        for k in range(2)
    ]
    packed = (a_train + jnp.concatenate(sides, 1)).astype(BF)
    for k in range(a_ref.shape[0]):
        a_ref[k] = packed


def score_kernel(
    a_ref, ao_ref, g_ref, go_ref, inv_ref, invo_ref, out_ref, inv_acc, *, Y, YL, L, wt, wq, d_part, group, n_g, n_d
):
    H, f_own, d_tile = g_ref.shape[0], g_ref.shape[2], n_d
    half = d_part // 2
    n = a_ref.shape[0]
    r, c = iota((n, n), 0), iota((n, n), 1)
    j = r % 16
    base = r - j + d_part
    unpack = [
        ((j >= k * half) & (j < (k + 1) * half) & (c == base + j - k * half)).astype(BF) for k in range(2)
    ]

    def query_acts(ref):
        width = ref.shape[1] // 2
        return (matmul(unpack[0], ref[:, :width]) + matmul(unpack[1], ref[:, width:])).astype(BF)

    def grads(ref, cols):
        return jnp.concatenate(
            [jnp.concatenate([ref[h, k, :, cols] for h in range(H)], 0) for k in range(L)], 1
        )

    qa = jnp.concatenate([query_acts(a_ref), query_acts(ao_ref)], 1)
    qg = jnp.concatenate([grads(g_ref, slice(wt, wt + wq)), grads(go_ref, slice(0, wq))], 1)
    g_train = grads(g_ref, slice(0, wt)).astype(F32)
    r, c = iota((d_tile, n), 0), iota((d_tile, n), 1)
    place = (c == (r // d_part) * 16 + r % d_part).astype(BF)
    me = lax.axis_index("zh")
    for s in range(H):
        rows = pl.ds(pl.multiple_of(lax.rem(me - s + H, H) * f_own, f_own), f_own)
        inv_acc[rows, :] = matmul(inv_ref[s, :, n_g:n_g + d_tile], place) + matmul(
            invo_ref[s, :, n_g:n_g + d_tile], place
        )
    inv = inv_acc[...]
    col = iota(qg.shape, 1)
    owner = (col // group) % (Y // YL) * YL + (col // (group * (Y // YL))) % YL
    acts = a_ref[...]
    for q in range(Y):
        raw = lax.dot_general(
            jnp.where(owner == q, qg, jnp.zeros_like(qg)), qa, (((1,), (1,)), ((), ())), preferred_element_type=F32
        )
        mixed = matmul((raw * inv).astype(BF), acts)
        out_ref[q:q + 1, :] = jnp.sum(mixed * g_train, axis=0, keepdims=True)


def staged_call(kernel, shapes, *args):
    whole = lambda v: pl.BlockSpec(v.shape, lambda i: (0,) * len(v.shape))
    return pl.pallas_call(
        kernel,
        grid=(1,),
        out_shape=shapes,
        in_specs=[whole(v) for v in args],
        out_specs=[whole(v) for v in shapes],
    )(*args)


def local_call(kernel, shapes, *args, scratch=()):
    return pl.pallas_call(
        kernel,
        out_shape=shapes,
        in_specs=[pl.BlockSpec(memory_space=pltpu.VMEM)] * len(args),
        out_specs=jax.tree.map(lambda _: pl.BlockSpec(memory_space=pltpu.VMEM), shapes),
        scratch_shapes=scratch,
        compiler_params=pltpu.CompilerParams(vmem_limit_bytes=40 * 2**20),
    )(*args)


def per_device(
    train_grads, train_acts, train_mask, query_grads, query_acts, grad_basis, act_basis, eigenvalues
):
    YH, YL, X, H, L, C = (lax.axis_size(a) for a in ("yh", "yl", "x", "zh", "zl", "c"))
    Y = YH * YL
    low = lax.axis_index("zl")
    gk, f_own = grad_basis.shape
    ak, d_own = act_basis.shape
    gs, as_ = gk // H, ak // H
    nt, nq = train_grads.shape[0], query_grads.shape[0]
    th, qh = nt // C, nq // C
    d_all = eigenvalues.shape[1]
    f_tile, d_block = f_own * H, d_own * H
    d_part = d_block // (H * L)
    d_tile = d_part * X * Y

    message = staged_call(
        functools.partial(message_kernel, H=H, L=L, C=C),
        [jax.ShapeDtypeStruct((YH, H * C * 2 * th, gs), BF)],
        train_grads, train_acts, train_mask.reshape(1, nt), query_grads, query_acts,
    )[0].reshape(YH * H * C, 2 * th, gs)
    message, grad_basis, act_basis, eigenvalues = lax.optimization_barrier(
        (message, grad_basis, act_basis, eigenvalues)
    )
    got = lax.all_to_all(message, ("yh", "zh", "c"), 0, 0, tiled=True)

    gb = grad_basis.T.reshape(f_own, H, gs).transpose(1, 0, 2)
    ab = act_basis.T
    main = ab[:, :H * LANES].reshape(d_own, H, LANES)
    rest = ab[:, H * LANES:].reshape(d_own, H, as_ - LANES)
    ab = jnp.concatenate([main.reshape(d_own, H, 4, -1), rest.reshape(d_own, H, 4, -1)], 3)
    ab = ab.transpose(1, 0, 2, 3).reshape(H, f_own, as_ // 4)

    inverse = 1.0 / (eigenvalues + damping)

    def wanted(c):
        h, rest = c // d_tile, c % d_tile
        return (rest // d_part) * d_block + h * (L * d_part) + low * d_part + rest % d_part

    sel = (wanted(iota((d_all, H * d_tile), 1)) == iota((d_all, H * d_tile), 0)).astype(BF)
    inv_high, inv_low = high_low(inverse)
    half = jnp.where(lax.axis_index("c") == 0, inv_high, inv_low)
    chosen = jnp.dot(half, sel, preferred_element_type=F32).astype(BF)
    chosen = chosen.reshape(f_own, H, d_tile).transpose(1, 0, 2)
    spare = -(gs + d_tile + as_ // 4) % LANES
    pieces = jnp.pad(jnp.concatenate([gb, chosen, ab], 2), ((0, 0), (0, 0), (0, spare)))
    got, pieces = lax.optimization_barrier((got, pieces))

    G = YH * H
    block = local_call(
        functools.partial(shuffle_kernel, G=G, th=th, qh=qh, gs=gs),
        jax.ShapeDtypeStruct((X * YL, G * C * (th + qh) + 16, gs + LANES), BF),
        got.reshape(G * C * 2 * th, gs),
    )
    full = lax.all_to_all(block, ("x", "yl"), 0, 0, tiled=True)
    own = jnp.stack([exchange(pieces, "zh", k) for k in range(H)])
    other = swap(own, "c")
    full, own, other = lax.optimization_barrier((full, own, other))

    tt, tq = G * th, G * qh
    wt, wq = X // L * YL * tt, X // L * YL * tq
    parts = local_call(
        functools.partial(rotate_kernel, H=H, L=L, tt=tt, tq=tq, gs=gs, f_own=f_own, d_part=d_part),
        jax.ShapeDtypeStruct((H * L, f_own + 32, wt + 2 * wq), BF),
        full, own, other,
    )
    parts = lax.all_to_all(parts, ("zh", "zl"), 0, 0, tiled=True)
    g_out, a_out = local_call(
        functools.partial(combine_kernel, n=H * L, f_own=f_own, L=L, wt=wt, wq=wq, d_part=d_part),
        (jax.ShapeDtypeStruct((f_own, wt + wq), BF), jax.ShapeDtypeStruct((Y * X, 16, L * wt), BF)),
        parts,
    )
    a_all = lax.all_to_all(a_out, ("yh", "yl", "x"), 0, 0, tiled=True).reshape(Y * X * 16, L * wt)
    g_all = lax.all_gather(lax.all_gather(g_out, "zl"), "zh")
    a_all, g_all = lax.optimization_barrier((a_all, g_all))
    a_other = swap(a_all, "c")
    g_other = swap(g_all[..., wt:], "c")
    scores = local_call(
        functools.partial(
            score_kernel, Y=Y, YL=YL, L=L, wt=wt, wq=wq, d_part=d_part, group=H * qh, n_g=gs, n_d=d_tile
        ),
        jax.ShapeDtypeStruct((Y, L * wt), F32),
        a_all, a_other, g_all, g_other, own, other,
        scratch=[pltpu.VMEM((f_tile, Y * X * 16), F32)],
    )
    n_out = Y * X * H * L
    scores = scores.T.reshape(n_out, scores.shape[1] // n_out * Y)
    mine = lax.all_to_all(scores, ("x", "yl", "yh", "zh", "zl"), 0, 0, tiled=True)
    return local_call(total_kernel, jax.ShapeDtypeStruct((scores.shape[1] // Y, Y), F32), mine)


def factored(mesh):
    devices = mesh.devices
    ex, blk = devices.shape
    yl, xs, zh, cores = 2, 4, 4, 2
    return Mesh(
        devices.reshape(ex // (yl * xs * zh), yl, xs, zh, blk // cores, cores), ("yh", "yl", "x", "zh", "zl", "c")
    )


def solution(mesh):
    ex, blk = ("yh", "yl", "x", "zh"), ("zl", "c")
    placed = (
        P(ex, blk),
        P(ex, blk),
        P(ex),
        P(ex, blk),
        P(ex, blk),
        P(blk, ex),
        P(blk, ex),
        P(ex, None),
    )
    return jax.shard_map(
        per_device, mesh=factored(mesh), in_specs=placed, out_specs=P(ex + blk, None), check_vma=False
    )
```

```python
import functools

import jax
import jax.numpy as jnp
from jax import lax
from jax.experimental import pallas as pl
from jax.experimental.pallas import tpu as pltpu
from jax.sharding import Mesh, PartitionSpec as P

damping = 0.1

BF = jnp.bfloat16
F32 = jnp.float32


def high_low(v):
    high = v.astype(BF)
    return high, (v - high.astype(F32)).astype(BF)


def swap(v, axis):
    return lax.ppermute(v, axis, [(0, 1), (1, 0)])


def exchange(pieces, axis, step):
    n = lax.axis_size(axis)
    out = lax.dynamic_index_in_dim(pieces, (lax.axis_index(axis) + step) % n, 0, keepdims=False)
    return out if step == 0 else lax.ppermute(out, axis, [(i, (i + step) % n) for i in range(n)])


def iota(shape, dim):
    return lax.broadcasted_iota(jnp.int32, shape, dim)


def matmul(a, b):
    return jnp.dot(a, b, preferred_element_type=F32)


def lanes(v, shift, start, stop):
    n = v.shape[1]
    if shift % n:
        v = pltpu.roll(v, shift % n, 1)
    c = iota(v.shape, 1)
    return jnp.where((c >= start) & (c < stop), v, 0.0)


LANES = 128


def message_kernel(tg_ref, ta_ref, mask_ref, qg_ref, qa_ref, out_ref, *, H, L, C):
    nt, nq = tg_ref.shape[0], qg_ref.shape[0]
    th, per = nt // C, nt // (L * C)
    rows = 2 * th * C

    def pick(n, row_of, upper):
        r, c = iota((rows, n), 0), iota((rows, n), 1)
        owner, k = r // (2 * th), r % th
        return ((r // th) % 2 == upper) & (row_of(owner, k) == c)

    def train(owner, k):
        return (k // per) * (C * per) + owner * per + k % per

    def query(owner, k):
        return owner * (nq // C) + k // 2

    masked = (pick(nt, train, 0).astype(F32) * mask_ref[...].astype(F32)).astype(BF)
    pick_q = pick(nq, query, 1).astype(BF)
    tg, ta = matmul(masked, tg_ref[...]), matmul(pick(nt, train, 1).astype(BF), ta_ref[...])
    qg, qa = matmul(pick_q, qg_ref[...]), matmul(pick_q, qa_ref[...])
    gs = tg.shape[1] // H
    wide = 3 * LANES
    low_half = iota((rows, wide), 0) % 2 == 0
    for h in range(H):
        q = qg[:, h * gs:(h + 1) * gs]
        q_high = jnp.concatenate([q[:, wide:], jnp.zeros((rows, 2 * wide - gs), F32)], 1)
        q = jnp.where(low_half, q[:, :wide], q_high)
        a_tile, rest = qa[:, h * LANES:(h + 1) * LANES], qa[:, H * LANES:]
        at = 32 * h
        b_tile = lanes(ta[:, H * LANES:], -at, 0, 32) + jnp.where(
            low_half[:, :LANES],
            lanes(a_tile, 32, 32, 96) + lanes(rest, 96 - at, 96, 112),
            lanes(a_tile, -32, 32, 96) + lanes(rest, 80 - at, 96, 112),
        )
        v = tg[:, h * gs:(h + 1) * gs] + jnp.concatenate([ta[:, h * LANES:(h + 1) * LANES], b_tile, q], 1)
        v = v.astype(BF)
        for y in range(out_ref.shape[0]):
            out_ref[y, h * rows:(h + 1) * rows] = v


def shuffle_kernel(got_ref, out_ref, *, G, th, qh, gs):
    core = lax.axis_index("c")
    n = got_ref.shape[0]
    each = 2 * th

    def pick(count, per, row_of):
        r, c = iota((count, n), 0), iota((count, n), 1)
        rest = r % (G * per)
        source = (core + r // (G * per)) % 2
        return (c == (rest // per) * (2 * each) + source * each + row_of(rest % per)).astype(BF)

    tn, qn = 2 * G * th, 2 * G * qh
    got = got_ref[...]
    t_grads = matmul(pick(tn, th, lambda k: k), got)
    t_acts = matmul(pick(tn, th, lambda k: th + k), got[:, :2 * LANES])
    q0, q1 = (matmul(pick(qn, qh, lambda k: th + 2 * k + half), got) for half in range(2))
    wide = 3 * LANES
    at = 2 * LANES
    q_grads = jnp.concatenate([q0[:, at:], q1[:, at:at + gs - wide]], 1)
    v0, v1 = q0[:, LANES:at], q1[:, LANES:at]
    q_a = lanes(v0, -32, 0, 64) + lanes(v1, 32, 64, 128)
    q_b = lanes(v0, 32, 0, 16) + lanes(v1, 48, 16, 32)
    body = jnp.concatenate(
        [jnp.concatenate([t_grads, t_acts[:, :LANES]], 1), jnp.concatenate([q_grads, q_a], 1)], 0
    ).astype(BF)
    tail = jnp.concatenate([t_acts[:, LANES:], q_b], 0)
    rows = tail.shape[0] // 4
    packed = sum(lanes(tail[g * rows:(g + 1) * rows], 32 * g, 32 * g, 32 * g + 32) for g in range(4)).astype(BF)
    packed = jnp.concatenate([packed[k:k + 16] for k in range(0, rows, 16)], 1)
    for x in range(out_ref.shape[0]):
        out_ref[x, :tn + qn] = body
        out_ref[x, tn + qn:, :packed.shape[1]] = packed


def total_kernel(parts_ref, out_ref):
    total = jnp.sum(parts_ref[...], axis=0, keepdims=True)
    width = out_ref.shape[1]
    for k in range(out_ref.shape[0]):
        out_ref[k:k + 1, :] = total[:, k * width:(k + 1) * width]


def rotate_kernel(full_ref, own_ref, other_ref, out_ref, *, H, L, tt, tq, gs, f_own, d_part):
    me = lax.axis_index("zh")
    per = 2 * (tt + tq)
    inner = full_ref.shape[0] // L
    wt, wq = inner * tt, inner * tq
    group = per // 4
    grads = [jnp.concatenate([b[s, :f_own, :gs] for s in range(H)], 0) for b in (own_ref, other_ref)]
    r, c = iota((H * L * 16, H * f_own), 0), iota((H * L * 16, H * f_own), 1)
    d = (r // 16) % L * d_part + r % 16
    picks = [((r % 16 < d_part) & (c == r // (16 * L) * f_own + d * 4 + q)).astype(BF) for q in range(4)]
    acts = []
    for b in (own_ref, other_ref):
        last = jnp.concatenate([b[s, :, b.shape[2] - LANES:] for s in range(H)], 0)
        v = [matmul(p, last) for p in picks]
        a_tile = sum(lanes(v[q], 32 * q - 64, 32 * q, 32 * q + 32) for q in range(4))
        b_tile = sum(lanes(v[q], 8 * q - 96, 8 * q, 8 * q + 8) for q in range(4))
        acts.append(jnp.concatenate([a_tile, b_tile], 1).astype(BF))
    r, c = iota((H * L * 32, H * L * 16), 0), iota((H * L * 32, H * L * 16), 1)
    repeat = ((r % 32 < (L + 1) * d_part) & (c == (r // 32) * 16 + (r % 32) % d_part)).astype(BF)
    acts = [matmul(repeat, v).astype(BF) for v in acts]
    a_parts = []
    for l in range(L):
        blocks = []
        for x in range(inner):
            at = l * inner + x
            packed = jnp.concatenate(
                [full_ref[at, per:, k * LANES:(k + 1) * LANES].astype(F32) for k in range(group // 16)], 0
            )
            tail = jnp.concatenate([lanes(packed, -32 * g, 0, 32) for g in range(4)], 0).astype(BF)
            blocks.append((full_ref.at[at], tail))
        g = a = 0.0
        for s in range(2):
            spans = [(b, t, s * tt, tt) for b, t in blocks] + [(b, t, 2 * tt + s * tq, tq) for b, t in blocks]
            tokens = jnp.concatenate([b[p:p + m, :gs] for b, _, p, m in spans], 0)
            inputs = jnp.concatenate(
                [jnp.concatenate([b[p:p + m, gs:], t[p:p + m]], 1) for b, t, p, m in spans], 0
            )
            g += lax.dot_general(grads[s], tokens, (((1,), (1,)), ((), ())), preferred_element_type=F32)
            a += lax.dot_general(acts[s], inputs, (((1,), (1,)), ((), ())), preferred_element_type=F32)
        a_parts.append(a)
        g_high, g_low = high_low(g[:, wt:])
        g_train = g[:, :wt].astype(BF)
        for s in range(H):
            m = l * H + lax.rem(me - s + H, H)
            out_ref[m, :f_own, :wt] = g_train[s * f_own:(s + 1) * f_own]
            out_ref[m, :f_own, wt:wt + wq] = g_high[s * f_own:(s + 1) * f_own]
            out_ref[m, :f_own, wt + wq:] = g_low[s * f_own:(s + 1) * f_own]
    merged = jnp.concatenate([a[:, wt:] for a in a_parts], 1)
    kind = (iota(merged.shape, 0) % 32) // d_part
    for l in range(L):
        merged = jnp.where(kind == l, a_parts[l][:, :wt], merged)
    a_high, a_low = high_low(merged)
    for s in range(H):
        for k in range(L):
            m = k * H + lax.rem(me - s + H, H)
            r = slice((s * L + k) * 32, (s * L + k + 1) * 32)
            out_ref[m, f_own:, :wt] = a_high[r]
            out_ref[m, f_own:, wt:] = a_low[r]


def combine_kernel(parts_ref, g_ref, a_ref, *, n, f_own, L, wt, wq, d_part):
    total = parts_ref[0].astype(F32)
    for k in range(1, n):
        total += parts_ref[k].astype(F32)
    g_train = total[:f_own, :wt].astype(BF)
    g_query = (total[:f_own, wt:wt + wq] + total[:f_own, wt + wq:]).astype(BF)
    g_ref[:, :wt] = g_train
    g_ref[:, wt:] = g_query
    act = total[f_own:, :wt] + total[f_own:, wt:]
    inside = iota((16, wt), 0) < d_part
    kinds = [jnp.where(inside, (pltpu.roll(act, 32 - k * d_part, 0) if k else act)[:16], 0.0) for k in range(L + 1)]
    a_train = jnp.concatenate(kinds[:L], 1)
    a_query = kinds[L].astype(BF)
    half = d_part // 2
    r = lax.broadcasted_iota(jnp.int32, (16, 16), 0)
    c = lax.broadcasted_iota(jnp.int32, (16, 16), 1)
    inside = (r >= d_part) & (r < d_part + half)
    sides = [
        jnp.dot((inside & (c == r - d_part + k * half)).astype(BF), a_query, preferred_element_type=F32)
        for k in range(2)
    ]
    packed = (a_train + jnp.concatenate(sides, 1)).astype(BF)
    for k in range(a_ref.shape[0]):
        a_ref[k] = packed


def score_kernel(
    a_ref, ao_ref, g_ref, go_ref, inv_ref, invo_ref, out_ref, inv_acc, *, Y, YL, L, wt, wq, d_part, group, n_g, n_d
):
    H, f_own, d_tile = g_ref.shape[0], g_ref.shape[2], n_d
    half = d_part // 2
    n = a_ref.shape[0]
    r, c = iota((n, n), 0), iota((n, n), 1)
    j = r % 16
    base = r - j + d_part
    unpack = [
        ((j >= k * half) & (j < (k + 1) * half) & (c == base + j - k * half)).astype(BF) for k in range(2)
    ]

    def query_acts(ref):
        width = ref.shape[1] // 2
        return (matmul(unpack[0], ref[:, :width]) + matmul(unpack[1], ref[:, width:])).astype(BF)

    def grads(ref, cols):
        return jnp.concatenate(
            [jnp.concatenate([ref[h, k, :, cols] for h in range(H)], 0) for k in range(L)], 1
        )

    qa = jnp.concatenate([query_acts(a_ref), query_acts(ao_ref)], 1)
    qg = jnp.concatenate([grads(g_ref, slice(wt, wt + wq)), grads(go_ref, slice(0, wq))], 1)
    g_train = grads(g_ref, slice(0, wt)).astype(F32)
    r, c = iota((d_tile, n), 0), iota((d_tile, n), 1)
    place = (c == (r // d_part) * 16 + r % d_part).astype(BF)
    me = lax.axis_index("zh")
    for s in range(H):
        rows = pl.ds(pl.multiple_of(lax.rem(me - s + H, H) * f_own, f_own), f_own)
        inv_acc[rows, :] = matmul(inv_ref[s, :, n_g:n_g + d_tile], place) + matmul(
            invo_ref[s, :, n_g:n_g + d_tile], place
        )
    inv = inv_acc[...]
    col = iota(qg.shape, 1)
    owner = (col // group) % (Y // YL) * YL + (col // (group * (Y // YL))) % YL
    acts = a_ref[...]
    for q in range(Y):
        raw = lax.dot_general(
            jnp.where(owner == q, qg, jnp.zeros_like(qg)), qa, (((1,), (1,)), ((), ())), preferred_element_type=F32
        )
        mixed = matmul((raw * inv).astype(BF), acts)
        out_ref[q:q + 1, :] = jnp.sum(mixed * g_train, axis=0, keepdims=True)


def staged_call(kernel, shapes, *args):
    whole = lambda v: pl.BlockSpec(v.shape, lambda i: (0,) * len(v.shape))
    return pl.pallas_call(
        kernel,
        grid=(1,),
        out_shape=shapes,
        in_specs=[whole(v) for v in args],
        out_specs=[whole(v) for v in shapes],
    )(*args)


def local_call(kernel, shapes, *args, scratch=()):
    return pl.pallas_call(
        kernel,
        out_shape=shapes,
        in_specs=[pl.BlockSpec(memory_space=pltpu.VMEM)] * len(args),
        out_specs=jax.tree.map(lambda _: pl.BlockSpec(memory_space=pltpu.VMEM), shapes),
        scratch_shapes=scratch,
        compiler_params=pltpu.CompilerParams(vmem_limit_bytes=40 * 2**20),
    )(*args)


def per_device(
    train_grads, train_acts, train_mask, query_grads, query_acts, grad_basis, act_basis, eigenvalues
):
    YH, YL, X, H, L, C = (lax.axis_size(a) for a in ("yh", "yl", "x", "zh", "zl", "c"))
    Y = YH * YL
    low = lax.axis_index("zl")
    gk, f_own = grad_basis.shape
    ak, d_own = act_basis.shape
    gs, as_ = gk // H, ak // H
    nt, nq = train_grads.shape[0], query_grads.shape[0]
    th, qh = nt // C, nq // C
    d_all = eigenvalues.shape[1]
    f_tile, d_block = f_own * H, d_own * H
    d_part = d_block // (H * L)
    d_tile = d_part * X * Y

    message = staged_call(
        functools.partial(message_kernel, H=H, L=L, C=C),
        [jax.ShapeDtypeStruct((YH, H * C * 2 * th, gs), BF)],
        train_grads, train_acts, train_mask.reshape(1, nt), query_grads, query_acts,
    )[0].reshape(YH * H * C, 2 * th, gs)
    message, grad_basis, act_basis, eigenvalues = lax.optimization_barrier(
        (message, grad_basis, act_basis, eigenvalues)
    )
    got = lax.all_to_all(message, ("yh", "zh", "c"), 0, 0, tiled=True)

    gb = grad_basis.T.reshape(f_own, H, gs).transpose(1, 0, 2)
    ab = act_basis.T
    main = ab[:, :H * LANES].reshape(d_own, H, LANES)
    rest = ab[:, H * LANES:].reshape(d_own, H, as_ - LANES)
    ab = jnp.concatenate([main.reshape(d_own, H, 4, -1), rest.reshape(d_own, H, 4, -1)], 3)
    ab = ab.transpose(1, 0, 2, 3).reshape(H, f_own, as_ // 4)

    inverse = 1.0 / (eigenvalues + damping)

    def wanted(c):
        h, rest = c // d_tile, c % d_tile
        return (rest // d_part) * d_block + h * (L * d_part) + low * d_part + rest % d_part

    sel = (wanted(iota((d_all, H * d_tile), 1)) == iota((d_all, H * d_tile), 0)).astype(BF)
    inv_high, inv_low = high_low(inverse)
    half = jnp.where(lax.axis_index("c") == 0, inv_high, inv_low)
    chosen = jnp.dot(half, sel, preferred_element_type=F32).astype(BF)
    chosen = chosen.reshape(f_own, H, d_tile).transpose(1, 0, 2)
    spare = -(gs + d_tile + as_ // 4) % LANES
    pieces = jnp.pad(jnp.concatenate([gb, chosen, ab], 2), ((0, 0), (0, 0), (0, spare)))
    got, pieces = lax.optimization_barrier((got, pieces))

    G = YH * H
    block = local_call(
        functools.partial(shuffle_kernel, G=G, th=th, qh=qh, gs=gs),
        jax.ShapeDtypeStruct((X * YL, G * C * (th + qh) + 16, gs + LANES), BF),
        got.reshape(G * C * 2 * th, gs),
    )
    full = lax.all_to_all(block, ("x", "yl"), 0, 0, tiled=True)
    own = jnp.stack([exchange(pieces, "zh", k) for k in range(H)])
    other = swap(own, "c")
    full, own, other = lax.optimization_barrier((full, own, other))

    tt, tq = G * th, G * qh
    wt, wq = X // L * YL * tt, X // L * YL * tq
    parts = local_call(
        functools.partial(rotate_kernel, H=H, L=L, tt=tt, tq=tq, gs=gs, f_own=f_own, d_part=d_part),
        jax.ShapeDtypeStruct((H * L, f_own + 32, wt + 2 * wq), BF),
        full, own, other,
    )
    parts = lax.all_to_all(parts, ("zl", "zh"), 0, 0, tiled=True)
    g_out, a_out = local_call(
        functools.partial(combine_kernel, n=H * L, f_own=f_own, L=L, wt=wt, wq=wq, d_part=d_part),
        (jax.ShapeDtypeStruct((f_own, wt + wq), BF), jax.ShapeDtypeStruct((Y * X, 16, L * wt), BF)),
        parts,
    )
    a_all = lax.all_to_all(a_out, ("yh", "yl", "x"), 0, 0, tiled=True).reshape(Y * X * 16, L * wt)
    g_all = lax.all_gather(lax.all_gather(g_out, "zl"), "zh")
    a_all, g_all = lax.optimization_barrier((a_all, g_all))
    a_other = swap(a_all, "c")
    g_other = swap(g_all[..., wt:], "c")
    scores = local_call(
        functools.partial(
            score_kernel, Y=Y, YL=YL, L=L, wt=wt, wq=wq, d_part=d_part, group=H * qh, n_g=gs, n_d=d_tile
        ),
        jax.ShapeDtypeStruct((Y, L * wt), F32),
        a_all, a_other, g_all, g_other, own, other,
        scratch=[pltpu.VMEM((f_tile, Y * X * 16), F32)],
    )
    n_out = Y * X * H * L
    scores = scores.T.reshape(n_out, scores.shape[1] // n_out * Y)
    mine = lax.all_to_all(scores, ("x", "yl", "yh", "zh", "zl"), 0, 0, tiled=True)
    return local_call(total_kernel, jax.ShapeDtypeStruct((scores.shape[1] // Y, Y), F32), mine)


def factored(mesh):
    devices = mesh.devices
    ex, blk = devices.shape
    yl, xs, zh, cores = 2, 4, 4, 2
    return Mesh(
        devices.reshape(ex // (yl * xs * zh), yl, xs, zh, blk // cores, cores), ("yh", "yl", "x", "zh", "zl", "c")
    )


def solution(mesh):
    ex, blk = ("yh", "yl", "x", "zh"), ("zl", "c")
    placed = (
        P(ex, blk),
        P(ex, blk),
        P(ex),
        P(ex, blk),
        P(ex, blk),
        P(blk, ex),
        P(blk, ex),
        P(ex, None),
    )
    return jax.shard_map(
        per_device, mesh=factored(mesh), in_specs=placed, out_specs=P(ex + blk, None), check_vma=False
    )
```
